32 devices in a mesh: ctx: 8 (over z, y), tp: 4 (over x, core).
Axes of the slice: x: 2, y: 2, z: 4, core: 2. Of those that a mesh axis runs over, the one named last changes fastest.
Arguments:
- projected: bfloat16 [1024, 4, 4640], P('ctx', 'tp'), may hold values from -6 to 6
- conv_weight: float32 [4, 4, 2560], P('tp'), may hold values from -3 to 3
- conv_bias: float32 [4, 2560], P('tp'), may hold values from -1.5 to 1.5
- step_bias: float32 [4, 32], P('tp'), may hold values from -1 to 0.5
- log_rates: float32 [4, 32], P('tp'), as said below
- norm_gain: float32 [4, 2048], P('tp'), may hold values from 0.1 to 1.9
- out_weight: bfloat16 [4, 2048, 4096], P('tp', 'ctx'), may hold values from -0.0625 to 0.0625
Outputs:
- mixed: bfloat16 [1024, 4096], P('ctx', 'tp')
The draws below stay inside these ranges and needn't reach their ends.
Inputs may be any that keep to these rules, and one draw needn't show every extreme that they name: log_rates lies between log(0.3 / 1024) and log(1 / 25).
All inputs are finite; a program needn't handle non-finite values.
Results may differ from the reference program's by a relative error of at most 0.0058.
Values may be sent and summed in bfloat16 or wider, within the bound.
A program may use at most 320 MiB of HBM per device.

```python
import math
import jax
import jax.numpy as jnp
from jax import lax

D = 4096
GROUPS = 4
HPG = 32
P_SIZE = 64
N = 256
KCONV = 4
SPAN = 128
TOKENS = 1024
GCH = 2048
GCONV = 2560
GCOLS = 4640


def draw_log_rates(key, part):
    slow_key, slow_rate_key, fast_key = jax.random.split(jax.random.fold_in(key, 7), 3)
    array_shape = (GROUPS, HPG)
    slow_share = 0.5
    slow_heads = jax.random.bernoulli(slow_key, slow_share, array_shape)
    slow_rates = jnp.exp(jax.random.uniform(slow_rate_key, array_shape, jnp.float32, math.log(0.3), math.log(2.0))) / TOKENS
    fast_rates = jnp.exp(jax.random.uniform(fast_key, array_shape, jnp.float32, math.log(1.0 / 50.0), math.log(1.0 / 25.0)))
    return jnp.log(jnp.where(slow_heads, slow_rates, fast_rates)).astype(jnp.float32)


def shard_levels(rng, extent, cuts, low, largest):
    def one(position, shards_of):
        draws = jax.random.uniform(jax.random.fold_in(jax.random.fold_in(rng, 6), position), (shards_of,), jnp.float32, low / len(cuts), largest / len(cuts))
        return jnp.repeat(jnp.exp(draws), extent[position] // shards_of).reshape((-1,) + (1,) * (len(extent) - position - 1))

    level = one(*cuts[0])
    for cut in cuts[1:]:
        level = level * one(*cut)
    return level


def normal_values(key, shape, scale, most, shards=(), kind=jnp.bfloat16):
    values = jax.random.normal(key, shape, jnp.float32) * scale
    if len(shards) > 0:
        values = shard_levels(key, shape, shards, -0.22, 0.18) * values
    return jnp.clip(values, min=-most, max=most).astype(kind)


def setup_inputs(seed: int = 0) -> dict:
    splits = jax.random.split(jax.random.key(seed), 8)
    return {
        "projected": normal_values(splits[0], (TOKENS, GROUPS, GCOLS), 1.0, 6.0, ((0, 8), (1, 4))),
        "conv_weight": normal_values(splits[1], (GROUPS, KCONV, GCONV), KCONV ** -0.5, 3.0, ((0, 4),), jnp.float32),
        "conv_bias": normal_values(splits[2], (GROUPS, GCONV), 0.3, 1.5, ((0, 4),), jnp.float32),
        "step_bias": jnp.clip(-1.0 + 1.5 * jax.random.uniform(splits[3], (GROUPS, HPG), jnp.float32) ** shard_levels(splits[3], (GROUPS, HPG), ((0, 4),), -0.2, 0.2), -1.0, 0.5),
        "log_rates": draw_log_rates(jax.random.fold_in(splits[7], 71), 0),
        "norm_gain": jnp.clip(1.0 + 0.18 * jax.random.normal(splits[5], (GROUPS, GCH), jnp.float32), 0.1, 1.9),
        "out_weight": normal_values(splits[6], (GROUPS, GCH, D), (GROUPS * GCH) ** -0.5, 0.0625, ((0, 4), (1, 8))),
    }


highest_precision = lax.Precision.HIGHEST

def ssd_blocks(inputs_x, step_sizes, decay_rate, b_rows, c_rows, block_rows):
    row_count = inputs_x.shape[0]
    block_count = row_count // block_rows
    head_count = inputs_x.shape[1]
    head_width = inputs_x.shape[2]
    state_count = b_rows.shape[1]
    x_blocks = inputs_x.reshape(block_count, block_rows, head_count, head_width)
    step_blocks = step_sizes.reshape(block_count, block_rows, head_count)
    b_blocks = b_rows.reshape(block_count, block_rows, state_count)
    c_blocks = c_rows.reshape(block_count, block_rows, state_count)
    causal_mask = (jnp.arange(block_rows)[:, None] >= jnp.arange(block_rows)[None, :])[None]

    def advance(carried, pieces):
        x_block, step_block, b_block, c_block = pieces
        log_steps = step_block * decay_rate[None, :]
        running = jnp.cumsum(log_steps, axis=0)
        intersection = jnp.dot(c_block, b_block.T, precision=highest_precision)
        log_gaps = running.T[:, :, None] - running.T[:, None, :]
        factors = jnp.where(causal_mask, jnp.exp(jnp.where(causal_mask, log_gaps, 0.0)), 0.0)
        factors = factors * intersection[None] * step_block.T[:, None, :]
        within = jnp.einsum('hts,shp->thp', factors, x_block, precision=highest_precision)
        carried_part = jnp.einsum('tn,hpn->thp', c_block, carried, precision=highest_precision) * jnp.exp(running)[:, :, None]
        tail_weight = jnp.exp(running[-1][None, :] - running) * step_block
        weighted = x_block * tail_weight[:, :, None]
        updated = carried * jnp.exp(running[-1])[:, None, None] + jnp.einsum('shp,sn->hpn', weighted, b_block, precision=highest_precision)
        return (updated, within + carried_part)
    initial = jnp.zeros((head_count, head_width, state_count), jnp.float32)
    final_state, outputs = lax.scan(advance, initial, (x_blocks, step_blocks, b_blocks, c_blocks))
    total_log = lax.optimization_barrier(jnp.sum(step_sizes * decay_rate[None, :], axis=0))
    return (outputs.reshape(row_count, head_count, head_width), final_state, total_log)

def reference(projected, conv_weight, conv_bias, step_bias, log_rates, norm_gain, out_weight):
    row_count = projected.shape[0]
    summed = jnp.zeros((row_count, D), jnp.float32)
    for group in range(GROUPS):
        conv_input = projected[:, group, GCH:GCH + GCONV].astype(jnp.float32)
        padded = jnp.concatenate([jnp.zeros((KCONV - 1, GCONV), jnp.float32), conv_input], axis=0)
        mixed_conv = conv_bias[group][None, :]
        for offset in range(KCONV):
            mixed_conv = mixed_conv + conv_weight[group, offset][None, :] * padded[offset:offset + row_count]
        activated = jax.nn.silu(mixed_conv).astype(jnp.bfloat16)
        step_sizes = jax.nn.softplus(projected[:, group, GCH + GCONV:].astype(jnp.float32) + step_bias[group][None, :])
        decay_rate = -jnp.exp(log_rates[group])
        values = activated[:, :GCH].astype(jnp.float32).reshape(row_count, HPG, P_SIZE)
        b_rows = activated[:, GCH:GCH + N].astype(jnp.float32)
        c_rows = activated[:, GCH + N:].astype(jnp.float32)
        outputs, final_state, total_log = ssd_blocks(values, step_sizes, decay_rate, b_rows, c_rows, SPAN)
        scanned = outputs.reshape(row_count, GCH).astype(jnp.bfloat16)
        gated = scanned.astype(jnp.float32) * jax.nn.silu(projected[:, group, :GCH].astype(jnp.float32))
        normed = (gated * lax.rsqrt(lax.optimization_barrier(jnp.mean(gated * gated, axis=1, keepdims=True)) + 1e-05) * norm_gain[group][None, :]).astype(jnp.bfloat16)
        summed = summed + jnp.dot(normed, out_weight[group], preferred_element_type=jnp.float32)
    return summed.astype(jnp.bfloat16)
```

```python
import jax
import jax.numpy as jnp
from jax import lax
from jax.sharding import PartitionSpec as P

P_SIZE = 64
N = 256
KCONV = 4
SPAN = 256
GCH = 2048
GCONV = 2560

F32 = jnp.float32
BF16 = jnp.bfloat16
highest_precision = lax.Precision.HIGHEST


def causal_conv(rows, weight, bias):
    count = rows.shape[0]
    padded = jnp.concatenate([jnp.zeros((KCONV - 1, rows.shape[1]), F32), rows.astype(F32)], axis=0)
    total = bias[None]
    for offset in range(KCONV):
        total = total + weight[offset][None] * padded[offset : offset + count]
    return jax.nn.silu(total).astype(BF16)


def ssd(values, steps, decay_rate, b_rows, c_rows, span):
    tokens, heads, width = values.shape
    blocks = tokens // span
    x = values.reshape(blocks, span, heads, width).transpose(0, 2, 1, 3)
    b_blocks = b_rows.reshape(blocks, span, N)
    c_blocks = c_rows.reshape(blocks, span, N)
    step = steps.reshape(blocks, span, heads).transpose(0, 2, 1)
    causal = jnp.arange(span)[:, None] >= jnp.arange(span)[None, :]
    running = jnp.einsum(
        "bhs,ts->bht", step * decay_rate[None, :, None], causal.astype(F32), precision=highest_precision
    )
    cross = jnp.einsum("btn,bsn->bts", c_blocks, b_blocks, preferred_element_type=F32)
    gaps = running[:, :, :, None] - running[:, :, None, :]
    factors = jnp.where(causal, jnp.exp(jnp.where(causal, gaps, 0.0)), 0.0)
    factors = (factors * cross[:, None] * step[:, :, None, :]).astype(BF16)
    within = jnp.einsum("bhts,bhsp->bhtp", factors, x, preferred_element_type=F32)
    tail = jnp.exp(running[:, :, -1:] - running) * step
    weighted = (x.astype(F32) * tail[..., None]).astype(BF16)
    added = jnp.einsum("bhsp,bsn->bhpn", weighted, b_blocks, preferred_element_type=F32)
    kept = jnp.exp(running[:, :, -1])

    def advance(state, piece):
        keep, add = piece
        return state * keep[:, None, None] + add, state

    _, entering = lax.scan(
        advance, jnp.zeros((heads, width, N), F32), (kept, added), unroll=min(blocks, 8)
    )
    carried = jnp.einsum("btn,bhpn->bhtp", c_blocks, entering.astype(BF16), preferred_element_type=F32)
    out = within + carried * jnp.exp(running)[..., None]
    return out.transpose(0, 2, 1, 3).reshape(tokens, heads * width)


def exchange(array, axis, bit):
    peers = lax.axis_size(axis)
    return lax.ppermute(array, axis, [(i, i ^ bit) for i in range(peers)])


def my_bit(axis, bit):
    return (lax.axis_index(axis) // bit) % 2


def bits_of(size):
    return [1 << i for i in range(size.bit_length() - 1)]


def on_device(projected, conv_weight, conv_bias, step_bias, log_rates, norm_gain, out_weight):
    rows = projected.shape[0]
    devices = lax.axis_size("ctx")
    tp = lax.axis_size("tp")
    me = lax.axis_index("ctx")
    width = GCH // devices
    heads = max(1, width // P_SIZE)
    here = projected[:, 0]

    parts = [
        jnp.concatenate(
            [here[:, d * width : (d + 1) * width], here[:, GCH + d * width : GCH + (d + 1) * width]], axis=1
        )
        for d in range(devices)
    ]
    moved = lax.all_to_all(jnp.stack(parts), "ctx", split_axis=0, concat_axis=0, tiled=True)
    tokens = devices * rows
    moved = moved.reshape(tokens, 2 * width)
    shared = lax.all_gather(here[:, 2 * GCH :], "ctx", axis=0, tiled=True)

    first = me * width
    values = causal_conv(
        moved[:, width:],
        lax.dynamic_slice_in_dim(conv_weight[0], first, width, axis=1),
        lax.dynamic_slice_in_dim(conv_bias[0], first, width),
    )
    keys = causal_conv(shared[:, : 2 * N], conv_weight[0, :, GCH:], conv_bias[0, GCH:])
    first_head = first // P_SIZE
    raw = lax.dynamic_slice_in_dim(shared[:, 2 * N :], first_head, heads, axis=1)
    bias = lax.dynamic_slice_in_dim(step_bias[0], first_head, heads)
    rate = -jnp.exp(lax.dynamic_slice_in_dim(log_rates[0], first_head, heads))
    steps = jax.nn.softplus(raw.astype(F32) + bias[None])
    scanned = ssd(
        values.reshape(tokens, heads, width // heads), steps, rate, keys[:, :N], keys[:, N:], SPAN
    ).astype(BF16)

    gated = scanned.astype(F32) * jax.nn.silu(moved[:, :width].astype(F32))
    squares = jnp.sum(gated * gated, axis=1).reshape(devices, rows)
    for bit in bits_of(devices):
        squares = squares + exchange(squares, "ctx", bit)
    scale = lax.rsqrt(squares.reshape(tokens, 1) / GCH + 1e-05)
    gain = lax.dynamic_slice_in_dim(norm_gain[0], first, width)
    normed = (gated * scale * gain[None]).astype(BF16)

    weight = out_weight[0]
    columns = weight.shape[1] // tp
    first_bit = 1
    mine = my_bit("tp", first_bit)

    def product(side, low, size):
        pieces = []
        for high in range(tp // 2):
            begin = (high * 2 + side) * columns + low
            block = lax.dynamic_slice_in_dim(weight, begin, size, axis=1)
            pieces.append(jnp.dot(normed, block, preferred_element_type=F32))
        return jnp.stack(pieces)

    tp_bits = [("tp", bit) for bit in bits_of(tp)[1:]]
    ctx_bits = [("ctx", bit) for bit in bits_of(devices)]
    near, far = ctx_bits[:1], ctx_bits[1:]
    orders = [tp_bits + near + far, near + far + tp_bits, far + tp_bits + near]
    unit = columns // 8
    sizes = [3 * unit, 3 * unit, 2 * unit]
    names = tp_bits[::-1] + ctx_bits[::-1]
    results = []
    low = 0
    for order, size in zip(orders, sizes):
        arrived = exchange(product(1 - mine, low, size).astype(BF16), "tp", first_bit)
        total = product(mine, low, size) + arrived.astype(F32)
        total = total.reshape((2,) * len(names) + (rows, size))
        left = list(names)
        for name in order:
            dim = left.index(name)
            side = my_bit(*name)
            away = lax.dynamic_index_in_dim(total, 1 - side, dim, keepdims=False).astype(BF16)
            stay = lax.dynamic_index_in_dim(total, side, dim, keepdims=False)
            total = stay + exchange(away, *name).astype(F32)
            left.remove(name)
        results.append(total)
        low += size
    return jnp.concatenate(results, axis=1).astype(BF16)


def solution(mesh):
    return jax.shard_map(
        on_device,
        mesh=mesh,
        in_specs=(
            P("ctx", "tp", None),
            P("tp", None, None),
            P("tp", None),
            P("tp", None),
            P("tp", None),
            P("tp", None),
            P("tp", "ctx", None),
        ),
        out_specs=P("ctx", "tp"),
        check_vma=False,
    )
```

```python
import jax
import jax.numpy as jnp
from jax import lax
from jax.sharding import PartitionSpec as P

P_SIZE = 64
N = 256
KCONV = 4
SPAN = 256
GCH = 2048
GCONV = 2560

F32 = jnp.float32
BF16 = jnp.bfloat16
highest_precision = lax.Precision.HIGHEST


def causal_conv(rows, weight, bias):
    count = rows.shape[0]
    padded = jnp.concatenate([jnp.zeros((KCONV - 1, rows.shape[1]), F32), rows.astype(F32)], axis=0)
    total = bias[None]
    for offset in range(KCONV):
        total = total + weight[offset][None] * padded[offset : offset + count]
    return jax.nn.silu(total).astype(BF16)


def ssd(values, steps, decay_rate, b_rows, c_rows, span):
    tokens, heads, width = values.shape
    blocks = tokens // span
    x = values.reshape(blocks, span, heads, width).transpose(0, 2, 1, 3)
    b_blocks = b_rows.reshape(blocks, span, N)
    c_blocks = c_rows.reshape(blocks, span, N)
    step = steps.reshape(blocks, span, heads).transpose(0, 2, 1)
    causal = jnp.arange(span)[:, None] >= jnp.arange(span)[None, :]
    running = jnp.einsum(
        "bhs,ts->bht", step * decay_rate[None, :, None], causal.astype(F32), precision=highest_precision
    )
    cross = jnp.einsum("btn,bsn->bts", c_blocks, b_blocks, preferred_element_type=F32)
    gaps = running[:, :, :, None] - running[:, :, None, :]
    factors = jnp.where(causal, jnp.exp(jnp.where(causal, gaps, 0.0)), 0.0)
    factors = (factors * cross[:, None] * step[:, :, None, :]).astype(BF16)
    within = jnp.einsum("bhts,bhsp->bhtp", factors, x, preferred_element_type=F32)
    tail = jnp.exp(running[:, :, -1:] - running) * step
    weighted = (x.astype(F32) * tail[..., None]).astype(BF16)
    added = jnp.einsum("bhsp,bsn->bhpn", weighted, b_blocks, preferred_element_type=F32)
    kept = jnp.exp(running[:, :, -1])

    def advance(state, piece):
        keep, add = piece
        return state * keep[:, None, None] + add, state

    _, entering = lax.scan(
        advance, jnp.zeros((heads, width, N), F32), (kept, added), unroll=min(blocks, 8)
    )
    carried = jnp.einsum("btn,bhpn->bhtp", c_blocks, entering.astype(BF16), preferred_element_type=F32)
    out = within + carried * jnp.exp(running)[..., None]
    return out.transpose(0, 2, 1, 3).reshape(tokens, heads * width)


def exchange(array, axis, bit):
    peers = lax.axis_size(axis)
    return lax.ppermute(array, axis, [(i, i ^ bit) for i in range(peers)])


def my_bit(axis, bit):
    return (lax.axis_index(axis) // bit) % 2


def bits_of(size):
    return [1 << i for i in range(size.bit_length() - 1)]


def gather_tokens(rows, order):
    whole = rows
    held = []
    for bit in order:
        other = exchange(whole, "ctx", bit)
        place = sum(1 for done in held if done > bit)
        own_first = jnp.stack([whole, other], axis=place)
        own_last = jnp.stack([other, whole], axis=place)
        whole = jnp.where(my_bit("ctx", bit) == 0, own_first, own_last)
        held.append(bit)
    return whole


def to_channels(columns, devices, me, width):
    rows = columns.shape[0]
    if devices > 8:
        pieces = columns.reshape(rows, devices, width).transpose(1, 0, 2)
        return lax.all_to_all(pieces, "ctx", split_axis=0, concat_axis=0, tiled=True).reshape(-1, width)
    whole = jnp.zeros((devices * rows, width), columns.dtype)
    for m in range(devices):
        piece = lax.dynamic_slice_in_dim(columns, (me ^ m) * width, width, axis=1)
        if m > 0:
            piece = exchange(piece, "ctx", m)
        whole = lax.dynamic_update_slice_in_dim(whole, piece, (me ^ m) * rows, axis=0)
    return whole


def on_device(projected, conv_weight, conv_bias, step_bias, log_rates, norm_gain, out_weight):
    rows = projected.shape[0]
    devices = lax.axis_size("ctx")
    tp = lax.axis_size("tp")
    me = lax.axis_index("ctx")
    width = GCH // devices
    heads = max(1, width // P_SIZE)
    here = projected[:, 0]

    tokens = devices * rows
    tail_columns = here[:, 2 * GCH :]
    orders = [bits_of(devices)[::-1], bits_of(devices)[::-1]]
    if devices > 2:
        orders[0] = orders[0][:1] + orders[0][1:][::-1]
    b_raw = gather_tokens(tail_columns[:, :N], orders[0]).reshape(tokens, N)
    rest_raw = gather_tokens(tail_columns[:, N:], orders[1]).reshape(tokens, -1)
    x_raw = to_channels(here[:, GCH : 2 * GCH], devices, me, width)
    z_raw = to_channels(here[:, :GCH], devices, me, width)

    first = me * width
    values = causal_conv(
        x_raw,
        lax.dynamic_slice_in_dim(conv_weight[0], first, width, axis=1),
        lax.dynamic_slice_in_dim(conv_bias[0], first, width),
    )
    b_keys = causal_conv(b_raw, conv_weight[0, :, GCH : GCH + N], conv_bias[0, GCH : GCH + N])
    c_keys = causal_conv(rest_raw[:, :N], conv_weight[0, :, GCH + N :], conv_bias[0, GCH + N :])
    first_head = first // P_SIZE
    raw = lax.dynamic_slice_in_dim(rest_raw[:, N:], first_head, heads, axis=1)
    bias = lax.dynamic_slice_in_dim(step_bias[0], first_head, heads)
    rate = -jnp.exp(lax.dynamic_slice_in_dim(log_rates[0], first_head, heads))
    steps = jax.nn.softplus(raw.astype(F32) + bias[None])
    scanned = ssd(
        values.reshape(tokens, heads, width // heads), steps, rate, b_keys, c_keys, SPAN
    ).astype(BF16)

    gated = scanned.astype(F32) * jax.nn.silu(z_raw.astype(F32))
    squares = jnp.sum(gated * gated, axis=1).reshape(devices, rows)
    radix = 1
    while radix < devices:
        reach = min(8, devices // radix)
        squares = squares + sum(exchange(squares, "ctx", radix * m) for m in range(1, reach))
        radix *= reach
    scale = lax.rsqrt(squares.reshape(tokens, 1) / GCH + 1e-05)
    gain = lax.dynamic_slice_in_dim(norm_gain[0], first, width)
    normed = (gated * scale * gain[None]).astype(BF16)

    weight = out_weight[0]
    columns = weight.shape[1] // tp
    first_bit = 1
    mine = my_bit("tp", first_bit)

    def product(side, low, size):
        pieces = []
        for high in range(tp // 2):
            begin = (high * 2 + side) * columns + low
            block = lax.dynamic_slice_in_dim(weight, begin, size, axis=1)
            pieces.append(jnp.dot(normed, block, preferred_element_type=F32))
        return jnp.stack(pieces)

    tp_bits = [("tp", bit) for bit in bits_of(tp)[1:]]
    ctx_bits = [("ctx", bit) for bit in bits_of(devices)]
    near, far = ctx_bits[:1], ctx_bits[1:]
    orders = [tp_bits + near + far, near + far + tp_bits, far + tp_bits + near]
    unit = columns // 8
    sizes = [3 * unit, 3 * unit, 2 * unit]
    names = tp_bits[::-1] + ctx_bits[::-1]
    lows = [0, sizes[0], sizes[0] + sizes[1]]
    leaving = [product(1 - mine, low, size).astype(BF16) for low, size in zip(lows, sizes)]
    arrived = lax.optimization_barrier([exchange(part, "tp", first_bit) for part in leaving])
    totals = [
        (product(mine, low, size) + part.astype(F32)).reshape((2,) * len(names) + (rows, size))
        for low, size, part in zip(lows, sizes, arrived)
    ]
    left = [list(names) for _ in orders]
    for stage in range(len(names)):
        aways, stays = [], []
        for index, order in enumerate(orders):
            name = order[stage]
            dim = left[index].index(name)
            side = my_bit(*name)
            away = lax.dynamic_index_in_dim(totals[index], 1 - side, dim, keepdims=False)
            aways.append(away.astype(BF16))
            stays.append(lax.dynamic_index_in_dim(totals[index], side, dim, keepdims=False))
            left[index].remove(name)
        aways = lax.optimization_barrier(aways)
        arrived = [exchange(away, *order[stage]) for away, order in zip(aways, orders)]
        arrived = lax.optimization_barrier(arrived)
        totals = [stay + part.astype(F32) for stay, part in zip(stays, arrived)]
    results = totals
    return jnp.concatenate(results, axis=1).astype(BF16)


def solution(mesh):
    return jax.shard_map(
        on_device,
        mesh=mesh,
        in_specs=(
            P("ctx", "tp", None),
            P("tp", None, None),
            P("tp", None),
            P("tp", None),
            P("tp", None),
            P("tp", None),
            P("tp", "ctx", None),
        ),
        out_specs=P("ctx", "tp"),
        check_vma=False,
    )
```

```python
import jax
import jax.numpy as jnp
from jax import lax
from jax.sharding import PartitionSpec as P

P_SIZE = 64
N = 256
KCONV = 4
SPAN = 256
GCH = 2048
GCONV = 2560

F32 = jnp.float32
BF16 = jnp.bfloat16
highest_precision = lax.Precision.HIGHEST


def causal_conv(rows, weight, bias):
    count = rows.shape[0]
    padded = jnp.concatenate([jnp.zeros((KCONV - 1, rows.shape[1]), F32), rows.astype(F32)], axis=0)
    total = bias[None]
    for offset in range(KCONV):
        total = total + weight[offset][None] * padded[offset : offset + count]
    return jax.nn.silu(total).astype(BF16)


def ssd(values, steps, decay_rate, b_rows, c_rows, span):
    tokens, heads, width = values.shape
    blocks = tokens // span
    x = values.reshape(blocks, span, heads, width).transpose(0, 2, 1, 3)
    b_blocks = b_rows.reshape(blocks, span, N)
    c_blocks = c_rows.reshape(blocks, span, N)
    step = steps.reshape(blocks, span, heads).transpose(0, 2, 1)
    causal = jnp.arange(span)[:, None] >= jnp.arange(span)[None, :]
    running = jnp.einsum(
        "bhs,ts->bht", step * decay_rate[None, :, None], causal.astype(F32), precision=highest_precision
    )
    cross = jnp.einsum("btn,bsn->bts", c_blocks, b_blocks, preferred_element_type=F32)
    gaps = running[:, :, :, None] - running[:, :, None, :]
    factors = jnp.where(causal, jnp.exp(jnp.where(causal, gaps, 0.0)), 0.0)
    factors = (factors * cross[:, None] * step[:, :, None, :]).astype(BF16)
    within = jnp.einsum("bhts,bhsp->bhtp", factors, x, preferred_element_type=F32)
    tail = jnp.exp(running[:, :, -1:] - running) * step
    weighted = (x.astype(F32) * tail[..., None]).astype(BF16)
    added = jnp.einsum("bhsp,bsn->bhpn", weighted, b_blocks, preferred_element_type=F32)
    kept = jnp.exp(running[:, :, -1])

    def advance(state, piece):
        keep, add = piece
        return state * keep[:, None, None] + add, state

    _, entering = lax.scan(
        advance, jnp.zeros((heads, width, N), F32), (kept, added), unroll=min(blocks, 8)
    )
    carried = jnp.einsum("btn,bhpn->bhtp", c_blocks, entering.astype(BF16), preferred_element_type=F32)
    out = within + carried * jnp.exp(running)[..., None]
    return out.transpose(0, 2, 1, 3).reshape(tokens, heads * width)


def exchange(array, axis, bit):
    peers = lax.axis_size(axis)
    return lax.ppermute(array, axis, [(i, i ^ bit) for i in range(peers)])


def my_bit(axis, bit):
    return (lax.axis_index(axis) // bit) % 2


def bits_of(size):
    return [1 << i for i in range(size.bit_length() - 1)]


def on_device(projected, conv_weight, conv_bias, step_bias, log_rates, norm_gain, out_weight):
    rows = projected.shape[0]
    devices = lax.axis_size("ctx")
    tp = lax.axis_size("tp")
    me = lax.axis_index("ctx")
    width = GCH // devices
    heads = max(1, width // P_SIZE)
    here = projected[:, 0]

    tail_columns, here = lax.optimization_barrier((here[:, 2 * GCH :], here))
    shared = lax.all_gather(tail_columns, "ctx", axis=0, tiled=True)
    parts = [
        jnp.concatenate(
            [here[:, d * width : (d + 1) * width], here[:, GCH + d * width : GCH + (d + 1) * width]], axis=1
        )
        for d in range(devices)
    ]
    moved = lax.all_to_all(jnp.stack(parts), "ctx", split_axis=0, concat_axis=0, tiled=True)
    tokens = devices * rows
    moved = moved.reshape(tokens, 2 * width)

    first = me * width
    values = causal_conv(
        moved[:, width:],
        lax.dynamic_slice_in_dim(conv_weight[0], first, width, axis=1),
        lax.dynamic_slice_in_dim(conv_bias[0], first, width),
    )
    keys = causal_conv(shared[:, : 2 * N], conv_weight[0, :, GCH:], conv_bias[0, GCH:])
    first_head = first // P_SIZE
    raw = lax.dynamic_slice_in_dim(shared[:, 2 * N :], first_head, heads, axis=1)
    bias = lax.dynamic_slice_in_dim(step_bias[0], first_head, heads)
    rate = -jnp.exp(lax.dynamic_slice_in_dim(log_rates[0], first_head, heads))
    steps = jax.nn.softplus(raw.astype(F32) + bias[None])
    scanned = ssd(
        values.reshape(tokens, heads, width // heads), steps, rate, keys[:, :N], keys[:, N:], SPAN
    ).astype(BF16)

    gated = scanned.astype(F32) * jax.nn.silu(moved[:, :width].astype(F32))
    squares = jnp.sum(gated * gated, axis=1).reshape(devices, rows)
    for bit in bits_of(devices):
        squares = squares + exchange(squares, "ctx", bit)
    scale = lax.rsqrt(squares.reshape(tokens, 1) / GCH + 1e-05)
    gain = lax.dynamic_slice_in_dim(norm_gain[0], first, width)
    normed = (gated * scale * gain[None]).astype(BF16)

    weight = out_weight[0]
    columns = weight.shape[1] // tp
    first_bit = 1
    mine = my_bit("tp", first_bit)

    def product(side, low, size):
        pieces = []
        for high in range(tp // 2):
            begin = (high * 2 + side) * columns + low
            block = lax.dynamic_slice_in_dim(weight, begin, size, axis=1)
            pieces.append(jnp.dot(normed, block, preferred_element_type=F32))
        return jnp.stack(pieces)

    tp_bits = [("tp", bit) for bit in bits_of(tp)[1:]]
    ctx_bits = [("ctx", bit) for bit in bits_of(devices)]
    near, far = ctx_bits[:1], ctx_bits[1:]
    orders = [tp_bits + near + far, near + far + tp_bits, far + tp_bits + near]
    unit = columns // 8
    sizes = [3 * unit, 3 * unit, 2 * unit]
    names = tp_bits[::-1] + ctx_bits[::-1]
    lows = [0, sizes[0], sizes[0] + sizes[1]]
    left = [list(names) for _ in orders]

    def halves(total, index, stage):
        name = orders[index][stage]
        dim = left[index].index(name)
        left[index].remove(name)
        side = my_bit(*name)
        away = lax.dynamic_index_in_dim(total, 1 - side, dim, keepdims=False).astype(BF16)
        return away, lax.dynamic_index_in_dim(total, side, dim, keepdims=False)

    aways, stays = [], []
    for index, (low, size) in enumerate(zip(lows, sizes)):
        arrived = exchange(product(1 - mine, low, size).astype(BF16), "tp", first_bit)
        total = product(mine, low, size) + arrived.astype(F32)
        away, stay = halves(total.reshape((2,) * len(names) + (rows, size)), index, 0)
        aways.append(away)
        stays.append(stay)
    aways = lax.optimization_barrier(aways)
    first_arrived = lax.optimization_barrier(
        [exchange(away, *order[0]) for away, order in zip(aways, orders)]
    )
    results = []
    for index, (stay, arrived) in enumerate(zip(stays, first_arrived)):
        total = stay + arrived.astype(F32)
        for stage in range(1, len(names)):
            away, stay = halves(total, index, stage)
            total = stay + exchange(away, *orders[index][stage]).astype(F32)
        results.append(total)
    return jnp.concatenate(results, axis=1).astype(BF16)


def solution(mesh):
    return jax.shard_map(
        on_device,
        mesh=mesh,
        in_specs=(
            P("ctx", "tp", None),
            P("tp", None, None),
            P("tp", None),
            P("tp", None),
            P("tp", None),
            P("tp", None),
            P("tp", "ctx", None),
        ),
        out_specs=P("ctx", "tp"),
        check_vma=False,
    )
```

```python
import jax
import jax.numpy as jnp
from jax import lax
from jax.sharding import PartitionSpec as P

P_SIZE = 64
N = 256
KCONV = 4
SPAN = 256
GCH = 2048
GCONV = 2560

F32 = jnp.float32
BF16 = jnp.bfloat16
highest_precision = lax.Precision.HIGHEST


def causal_conv(rows, weight, bias):
    count = rows.shape[0]
    padded = jnp.concatenate([jnp.zeros((KCONV - 1, rows.shape[1]), F32), rows.astype(F32)], axis=0)
    total = bias[None]
    for offset in range(KCONV):
        total = total + weight[offset][None] * padded[offset : offset + count]
    return jax.nn.silu(total).astype(BF16)


def ssd(values, steps, decay_rate, b_rows, c_rows, span):
    tokens, heads, width = values.shape
    blocks = tokens // span
    x = values.reshape(blocks, span, heads, width).transpose(0, 2, 1, 3)
    b_blocks = b_rows.reshape(blocks, span, N)
    c_blocks = c_rows.reshape(blocks, span, N)
    step = steps.reshape(blocks, span, heads).transpose(0, 2, 1)
    causal = jnp.arange(span)[:, None] >= jnp.arange(span)[None, :]
    running = jnp.einsum(
        "bhs,ts->bht", step * decay_rate[None, :, None], causal.astype(F32), precision=highest_precision
    )
    cross = jnp.einsum("btn,bsn->bts", c_blocks, b_blocks, preferred_element_type=F32)
    gaps = running[:, :, :, None] - running[:, :, None, :]
    factors = jnp.where(causal, jnp.exp(jnp.where(causal, gaps, 0.0)), 0.0)
    factors = (factors * cross[:, None] * step[:, :, None, :]).astype(BF16)
    within = jnp.einsum("bhts,bhsp->bhtp", factors, x, preferred_element_type=F32)
    tail = jnp.exp(running[:, :, -1:] - running) * step
    weighted = (x.astype(F32) * tail[..., None]).astype(BF16)
    added = jnp.einsum("bhsp,bsn->bhpn", weighted, b_blocks, preferred_element_type=F32)
    kept = jnp.exp(running[:, :, -1])

    def advance(state, piece):
        keep, add = piece
        return state * keep[:, None, None] + add, state

    _, entering = lax.scan(
        advance, jnp.zeros((heads, width, N), F32), (kept, added), unroll=min(blocks, 8)
    )
    carried = jnp.einsum("btn,bhpn->bhtp", c_blocks, entering.astype(BF16), preferred_element_type=F32)
    out = within + carried * jnp.exp(running)[..., None]
    return out.transpose(0, 2, 1, 3).reshape(tokens, heads * width)


def exchange(array, axis, bit):
    peers = lax.axis_size(axis)
    return lax.ppermute(array, axis, [(i, i ^ bit) for i in range(peers)])


def my_bit(axis, bit):
    return (lax.axis_index(axis) // bit) % 2


def bits_of(size):
    return [1 << i for i in range(size.bit_length() - 1)]


def gather_tokens(rows, order):
    whole = rows
    held = []
    for bit in order:
        other = exchange(whole, "ctx", bit)
        place = sum(1 for done in held if done > bit)
        own_first = jnp.stack([whole, other], axis=place)
        own_last = jnp.stack([other, whole], axis=place)
        whole = jnp.where(my_bit("ctx", bit) == 0, own_first, own_last)
        held.append(bit)
    return whole


def on_device(projected, conv_weight, conv_bias, step_bias, log_rates, norm_gain, out_weight):
    rows = projected.shape[0]
    devices = lax.axis_size("ctx")
    tp = lax.axis_size("tp")
    me = lax.axis_index("ctx")
    width = GCH // devices
    heads = max(1, width // P_SIZE)
    here = projected[:, 0]

    tail_columns, here = lax.optimization_barrier((here[:, 2 * GCH :], here))
    shared = gather_tokens(tail_columns, bits_of(devices)[::-1])
    shared = shared.reshape(devices * rows, tail_columns.shape[1])
    parts = [
        jnp.concatenate(
            [here[:, d * width : (d + 1) * width], here[:, GCH + d * width : GCH + (d + 1) * width]], axis=1
        )
        for d in range(devices)
    ]
    moved = lax.all_to_all(jnp.stack(parts), "ctx", split_axis=0, concat_axis=0, tiled=True)
    tokens = devices * rows
    moved = moved.reshape(tokens, 2 * width)

    first = me * width
    values = causal_conv(
        moved[:, width:],
        lax.dynamic_slice_in_dim(conv_weight[0], first, width, axis=1),
        lax.dynamic_slice_in_dim(conv_bias[0], first, width),
    )
    keys = causal_conv(shared[:, : 2 * N], conv_weight[0, :, GCH:], conv_bias[0, GCH:])
    first_head = first // P_SIZE
    raw = lax.dynamic_slice_in_dim(shared[:, 2 * N :], first_head, heads, axis=1)
    bias = lax.dynamic_slice_in_dim(step_bias[0], first_head, heads)
    rate = -jnp.exp(lax.dynamic_slice_in_dim(log_rates[0], first_head, heads))
    steps = jax.nn.softplus(raw.astype(F32) + bias[None])
    scanned = ssd(
        values.reshape(tokens, heads, width // heads), steps, rate, keys[:, :N], keys[:, N:], SPAN
    ).astype(BF16)

    gated = scanned.astype(F32) * jax.nn.silu(moved[:, :width].astype(F32))
    squares = jnp.sum(gated * gated, axis=1).reshape(devices, rows)
    for bit in bits_of(devices):
        squares = squares + exchange(squares, "ctx", bit)
    scale = lax.rsqrt(squares.reshape(tokens, 1) / GCH + 1e-05)
    gain = lax.dynamic_slice_in_dim(norm_gain[0], first, width)
    normed = (gated * scale * gain[None]).astype(BF16)

    weight = out_weight[0]
    columns = weight.shape[1] // tp
    first_bit = 1
    mine = my_bit("tp", first_bit)

    def product(side, low, size):
        pieces = []
        for high in range(tp // 2):
            begin = (high * 2 + side) * columns + low
            block = lax.dynamic_slice_in_dim(weight, begin, size, axis=1)
            pieces.append(jnp.dot(normed, block, preferred_element_type=F32))
        return jnp.stack(pieces)

    tp_bits = [("tp", bit) for bit in bits_of(tp)[1:]]
    ctx_bits = [("ctx", bit) for bit in bits_of(devices)]
    near, far = ctx_bits[:1], ctx_bits[1:]
    orders = [tp_bits + near + far, near + far + tp_bits, far + tp_bits + near]
    unit = columns // 8
    sizes = [3 * unit, 3 * unit, 2 * unit]
    names = tp_bits[::-1] + ctx_bits[::-1]
    lows = [0, sizes[0], sizes[0] + sizes[1]]
    left = [list(names) for _ in orders]

    def halves(total, index, stage):
        name = orders[index][stage]
        dim = left[index].index(name)
        left[index].remove(name)
        side = my_bit(*name)
        away = lax.dynamic_index_in_dim(total, 1 - side, dim, keepdims=False).astype(BF16)
        return away, lax.dynamic_index_in_dim(total, side, dim, keepdims=False)

    aways, stays = [], []
    for index, (low, size) in enumerate(zip(lows, sizes)):
        arrived = exchange(product(1 - mine, low, size).astype(BF16), "tp", first_bit)
        total = product(mine, low, size) + arrived.astype(F32)
        away, stay = halves(total.reshape((2,) * len(names) + (rows, size)), index, 0)
        aways.append(away)
        stays.append(stay)
    aways = lax.optimization_barrier(aways)
    first_arrived = lax.optimization_barrier(
        [exchange(away, *order[0]) for away, order in zip(aways, orders)]
    )
    results = []
    for index, (stay, arrived) in enumerate(zip(stays, first_arrived)):
        total = stay + arrived.astype(F32)
        for stage in range(1, len(names)):
            away, stay = halves(total, index, stage)
            total = stay + exchange(away, *orders[index][stage]).astype(F32)
        results.append(total)
    return jnp.concatenate(results, axis=1).astype(BF16)


def solution(mesh):
    return jax.shard_map(
        on_device,
        mesh=mesh,
        in_specs=(
            P("ctx", "tp", None),
            P("tp", None, None),
            P("tp", None),
            P("tp", None),
            P("tp", None),
            P("tp", None),
            P("tp", "ctx", None),
        ),
        out_specs=P("ctx", "tp"),
        check_vma=False,
    )
```
